32 devices in a mesh: row: 8 (over y, x, core), col: 4 (over z).
Axes of the slice: x: 2, y: 2, z: 4, core: 2. Of those that a mesh axis runs over, the one named last changes fastest.
Arguments:
- field: float32 [1, 256, 256, 512], P(None, 'row', 'col'), may hold values from -6 to 6
- shell: int32 [256, 256, 256], P(('row', 'col')), may hold values from 0 to 255
Outputs:
- power_modes: float32 [1, 256, 256, 256], P(None, ('row', 'col'))
- spectrum: float32 [1, 256], replicated
The draws below stay inside these ranges and needn't reach their ends.
All inputs are finite; a program needn't handle non-finite values.
Results may differ from the reference program's by a relative error of at most 0.0003.
Values sent between devices are 32-bit elements; how exact they have to be, the bound alone decides.
A program may use at most 64 MiB of HBM per device.

```python
import math
import jax
import jax.numpy as jnp
import numpy as np
from jax import lax

NX = 256
NY = 256
NZ = 512
SHELLS = 256
FIELDS = 1
KZ = 256


def place_ends(entries, own_key, smallest, top_value):
    index_at = [jax.random.randint(jax.random.fold_in(own_key, axis), (), 0, length) for axis, length in enumerate(entries.shape)]
    longest = entries.shape.index(max(entries.shape))
    next_to = index_at[:longest] + [(index_at[longest] + 1) % entries.shape[longest]] + index_at[longest + 1:]
    return entries.at[tuple(index_at)].set(smallest).at[tuple(next_to)].set(top_value)


def steps_of(stream_key, extent, pieces, low, top_value):
    level, own = 1.0, jax.random.fold_in(stream_key, 6)
    for dim, parts in pieces:
        steps = jnp.exp(jax.random.uniform(jax.random.fold_in(own, dim), (parts,), jnp.float32, low / len(pieces), top_value / len(pieces)))
        level = level * jnp.repeat(steps, extent[dim] // parts).reshape([-1 if axis == dim else 1 for axis in range(len(extent))])
    return level


def rank_bounds(number_of, lean):
    loads = [(1 << 20) // math.isqrt(standing ** lean) + 1 for standing in range(1, number_of + 1)]
    spread = 1 + sum(loads) // (1 << 30)
    return np.cumsum(np.array([max(1, weight // spread) for weight in loads]))


def skewed_ids(stream_key, dims, amount, skew):
    listing = rank_bounds(amount, skew)
    pick = jax.random.randint(jax.random.fold_in(stream_key, 1), dims, 0, int(listing[amount - 1]))
    grade = jnp.searchsorted(jnp.asarray(listing, jnp.int32), pick, side="right")
    return jax.random.permutation(jax.random.fold_in(stream_key, 2), amount)[grade].astype(jnp.int32)


def scatter_about(rng, dims, width, limit, pieces=(), held_as=jnp.bfloat16):
    factor_of = steps_of(rng, dims, pieces, -0.22, 0.18) if pieces else 1.0
    drawn = jax.random.normal(rng, dims, jnp.float32) * width * factor_of
    return jnp.minimum(jnp.maximum(drawn, -limit), limit).astype(held_as)


def setup_inputs(seed: int = 0) -> dict:
    splits = jax.random.split(jax.random.key(seed), 3)
    field = scatter_about(splits[0], (FIELDS, NX, NY, NZ), 1.0, 6.0, ((1, 8), (2, 4)), jnp.float32)
    shell = place_ends(skewed_ids(splits[1], (KZ, NY, NX), SHELLS, 1), jax.random.fold_in(splits[1], 3), 0, SHELLS - 1).astype(jnp.int32)
    return dict(field=field, shell=shell)


def transform_one(single):
    spec = jnp.fft.rfftn(single)[:, :, :KZ]
    power = (jnp.real(spec) ** 2 + jnp.imag(spec) ** 2) / (NX * NY * NZ)
    return jnp.transpose(power, (2, 1, 0)).astype(jnp.float32)


def reference(field, shell):
    power_modes = lax.map(transform_one, field)
    labels = shell.reshape(-1).astype(jnp.int32)
    rows = []
    for index in range(FIELDS):
        sums = jax.ops.segment_sum(power_modes[index].reshape(-1), labels, num_segments=SHELLS)
        rows.append(sums)
    spectrum = (jnp.stack(rows) * (SHELLS / (KZ * NY * NX))).astype(jnp.float32)
    return power_modes, spectrum
```

```python
import math

import functools

import jax
import jax.numpy as jnp
import numpy as np
from jax import lax
from jax.experimental import pallas as pl
from jax.experimental.pallas import tpu as pltpu
from jax.sharding import PartitionSpec as P

SHELLS = 256


HIGH = lax.Precision.HIGHEST


def tables(length, freqs):
    places = lax.iota(jnp.int32, length)
    phase = places[:, None] * freqs[None, :] % length
    angle = phase.astype(jnp.float32) * (2.0 * math.pi / length)
    factor = 1.0 / math.sqrt(length)
    return (jnp.cos(angle) * factor, -jnp.sin(angle) * factor)


def split_three(values):
    upper = values.astype(jnp.bfloat16)
    upper_back = lax.optimization_barrier(upper).astype(jnp.float32)
    rest = values - upper_back
    middle = rest.astype(jnp.bfloat16)
    middle_back = lax.optimization_barrier(middle).astype(jnp.float32)
    lowest = (rest - middle_back).astype(jnp.bfloat16)
    return jnp.concatenate([upper, middle, lowest], axis=0)


def general(field, shell):
    fields, cx, cy, nz = field.shape
    n_row = lax.axis_size("row")
    n_col = lax.axis_size("col")
    nx = cx * n_row
    ny = cy * n_col
    keep = nz // 2
    planes = keep // (n_row * n_col)
    cos_x, sin_x = tables(nx, lax.iota(jnp.int32, nx))
    cos_y, sin_y = tables(ny, lax.iota(jnp.int32, ny))
    slots = lax.iota(jnp.int32, keep)
    col_block = slots // (n_row * planes)
    row_block = slots // planes % n_row
    inner = slots % planes
    freqs = (row_block * n_col + col_block) * planes + inner
    cos_z, sin_z = tables(nz, freqs)
    real = jnp.einsum("fxyz,zk->fxyk", field, cos_z, precision=HIGH)
    imag = jnp.einsum("fxyz,zk->fxyk", field, sin_z, precision=HIGH)
    cos_four = cos_y.reshape(n_col, cy, ny)
    sin_four = sin_y.reshape(n_col, cy, ny)
    a_re = lax.all_to_all(real, "col", split_axis=3, concat_axis=3, tiled=True)
    a_im = lax.all_to_all(imag, "col", split_axis=3, concat_axis=3, tiled=True)
    count = a_re.shape[1]
    a_re = a_re.reshape(fields, count, cy, n_col, keep // n_col)
    a_im = a_im.reshape(fields, count, cy, n_col, keep // n_col)
    o_re = jnp.einsum("fiasm,sak->fimk", a_re, cos_four, precision=HIGH) - jnp.einsum(
        "fiasm,sak->fimk", a_im, sin_four, precision=HIGH
    )
    o_im = jnp.einsum("fiasm,sak->fimk", a_re, sin_four, precision=HIGH) + jnp.einsum(
        "fiasm,sak->fimk", a_im, cos_four, precision=HIGH
    )
    real = o_re
    imag = o_im
    b_re = lax.all_to_all(real, "row", split_axis=2, concat_axis=1, tiled=True)
    b_im = lax.all_to_all(imag, "row", split_axis=2, concat_axis=1, tiled=True)
    o_re = jnp.einsum("fxpi,xk->fpik", b_re, cos_x, precision=HIGH) - jnp.einsum(
        "fxpi,xk->fpik", b_im, sin_x, precision=HIGH
    )
    o_im = jnp.einsum("fxpi,xk->fpik", b_re, sin_x, precision=HIGH) + jnp.einsum(
        "fxpi,xk->fpik", b_im, cos_x, precision=HIGH
    )
    power = o_re * o_re + o_im * o_im
    total = planes * ny * nx
    width = math.gcd(total, 32768)
    flat = power.reshape(fields, total)
    labels = shell.reshape(total)
    shell_ids = lax.iota(jnp.int32, SHELLS)

    def add_block(index, summed):
        start = index * width
        part = lax.dynamic_slice_in_dim(flat, start, width, 1)
        marks = lax.dynamic_slice_in_dim(labels, start, width, 0)
        onehot = (marks[:, None] == shell_ids[None, :]).astype(jnp.bfloat16)
        pieces = split_three(part)
        return summed + jnp.dot(pieces, onehot, preferred_element_type=jnp.float32)

    stacked = lax.fori_loop(
        0, total // width, add_block, jnp.zeros((3 * fields, SHELLS), jnp.float32)
    )
    sums = jnp.sum(stacked.reshape(3, fields, SHELLS), axis=0)
    sums = lax.psum(sums, ("row", "col"))
    spectrum = sums * (float(SHELLS) / (keep * ny * nx))
    return (power, spectrum)


F32 = jnp.float32
BF16 = jnp.bfloat16
MIB = 1 << 20
STEP = 8
HALF = 16


def waves(length, freqs):
    phase = np.arange(length)[:, None] * np.asarray(freqs)[None, :] % length
    angle = phase * (2.0 * np.pi / length)
    factor = 1.0 / math.sqrt(length)
    return np.cos(angle) * factor, np.sin(angle) * factor


def two_parts(table):
    upper = table.astype(np.float32).astype(jnp.bfloat16)
    lower = (table - upper.astype(np.float64)).astype(np.float32).astype(jnp.bfloat16)
    return upper, lower


def halves(values):
    upper = values.astype(BF16)
    return upper, (values - upper.astype(F32)).astype(BF16)


def dot(a, b):
    return jnp.dot(a, b, preferred_element_type=F32)


def product(a, b):
    return dot(a[0], b[0]) + (dot(a[1], b[0]) + dot(a[0], b[1]))


def greet(n_row, n_col, my_row, my_col):
    barrier = pltpu.get_barrier_semaphore()
    for k in range(1, n_col):
        pl.semaphore_signal(
            barrier, inc=1, device_id={"col": lax.rem(my_col + k, n_col)}, device_id_type=pl.DeviceIdType.MESH
        )
    for k in range(1, n_row):
        pl.semaphore_signal(
            barrier, inc=1, device_id={"row": lax.rem(my_row + k, n_row)}, device_id_type=pl.DeviceIdType.MESH
        )
    pl.semaphore_wait(barrier, n_col + n_row - 2)


def exchange_kernel(n_row, n_col, planes, f_ref, tzh, tzl, tyh, tyl, out_ref, snd1, rcv1, snd2, s1, r1, s2, r2, own):
    my_row = lax.axis_index("row")
    my_col = lax.axis_index("col")
    cx, cy, nz = f_ref.shape
    ny = cy * n_col
    width = rcv1.shape[3]
    half = width // 2
    steps = cx // STEP

    def col_copy(q, k):
        xs = pl.ds(pl.multiple_of(q * STEP, STEP), STEP)
        dest = lax.rem(my_col + k, n_col)
        return pltpu.make_async_remote_copy(
            src_ref=snd1.at[dest, xs],
            dst_ref=rcv1.at[my_col, xs],
            send_sem=s1.at[q, k],
            recv_sem=r1.at[q, k],
            device_id={"col": dest},
            device_id_type=pl.DeviceIdType.MESH,
        )

    def row_copy(q, k):
        dest = lax.rem(my_row + k, n_row)
        there = pl.ds(pl.multiple_of(my_row * cx + q * STEP, STEP), STEP)
        return pltpu.make_async_remote_copy(
            src_ref=snd2.at[dest, :, :, pl.ds(pl.multiple_of(q * STEP, STEP), STEP)],
            dst_ref=out_ref.at[:, :, there],
            send_sem=s2.at[q, k],
            recv_sem=r2.at[q, k],
            device_id={"row": dest},
            device_id_type=pl.DeviceIdType.MESH,
        )

    def own_copy(q):
        there = pl.ds(pl.multiple_of(my_row * cx + q * STEP, STEP), STEP)
        return pltpu.make_async_copy(
            snd2.at[my_row, :, :, pl.ds(pl.multiple_of(q * STEP, STEP), STEP)], out_ref.at[:, :, there], own.at[q]
        )

    greet(n_row, n_col, my_row, my_col)

    def depth_step(q, carry):
        xs = pl.ds(pl.multiple_of(q * STEP, STEP), STEP)
        data = halves(f_ref[xs].reshape(STEP * cy, nz))
        for c in range(n_col):
            cs = slice(c * width, (c + 1) * width)
            res = product(data, (tzh[:, cs], tzl[:, cs]))
            snd1[c, xs] = res.reshape(STEP, cy, width)
        for k in range(n_col - 1, 0, -1):
            col_copy(q, k).start()
        rcv1[my_col, xs] = snd1[my_col, xs]
        return carry

    lax.fori_loop(0, steps, depth_step, 0)

    def second_step(q, carry):
        for k in range(1, n_col):
            col_copy(q, k).wait_recv()
        parts = []
        for i in range(STEP):
            block = jnp.concatenate([rcv1[s, q * STEP + i] for s in range(n_col)], axis=0)
            parts.append(block.T)
        data = halves(jnp.concatenate(parts, axis=0))
        res = product(data, (tyh[...], tyl[...])).reshape(STEP, width, 2 * ny)
        real = res[:, :half, :ny] + res[:, half:, ny:]
        imag = res[:, half:, :ny] - res[:, :half, ny:]
        xs = pl.ds(pl.multiple_of(q * STEP, STEP), STEP)
        snd2[:, :, 0, xs] = jnp.swapaxes(real, 0, 1).reshape(n_row, planes, STEP, ny)
        snd2[:, :, 1, xs] = jnp.swapaxes(imag, 0, 1).reshape(n_row, planes, STEP, ny)
        for k in range(n_row - 1, 0, -1):
            row_copy(q, k).start()
        own_copy(q).start()
        return carry

    lax.fori_loop(0, steps, second_step, 0)

    def finish(q, carry):
        for k in range(1, n_col):
            col_copy(q, k).wait_send()
        for k in range(1, n_row):
            row_copy(q, k).wait()
        own_copy(q).wait()
        return carry

    lax.fori_loop(0, steps, finish, 0)


def exchange(field, n_row, n_col, planes):
    cx, cy, nz = field.shape
    nx, ny, keep = cx * n_row, cy * n_col, nz // 2
    width = 2 * keep // n_col
    order = []
    for c in range(n_col):
        order.append([(r * n_col + c) * planes + p for r in range(n_row) for p in range(planes)])
    columns = []
    for freqs in order:
        cos_z, sin_z = waves(nz, freqs)
        columns += [cos_z, -sin_z]
    tz = two_parts(np.concatenate(columns, axis=1))
    ty = two_parts(np.concatenate(waves(ny, np.arange(ny)), axis=1))
    steps = cx // STEP
    vmem = pl.BlockSpec(memory_space=pltpu.VMEM)
    dma = pltpu.SemaphoreType.DMA
    flops = 6 * (cx * cy * nz * 2 * keep + cx * width * ny * 2 * ny)
    return pl.pallas_call(
        functools.partial(exchange_kernel, n_row, n_col, planes),
        out_shape=jax.ShapeDtypeStruct((planes, 2, nx, ny), F32),
        in_specs=[vmem] * 5,
        out_specs=pl.BlockSpec(memory_space=pl.ANY),
        scratch_shapes=[
            pltpu.VMEM((n_col, cx, cy, width), F32),
            pltpu.VMEM((n_col, cx, cy, width), F32),
            pltpu.VMEM((n_row, planes, 2, cx, ny), F32),
            dma((steps, n_col)),
            dma((steps, n_col)),
            dma((steps, n_row)),
            dma((steps, n_row)),
            dma((steps,)),
        ],
        compiler_params=pltpu.CompilerParams(
            collective_id=0, has_side_effects=True, vmem_limit_bytes=48 * MIB
        ),
        cost_estimate=pl.CostEstimate(flops=flops, bytes_accessed=8 * cx * cy * nz, transcendentals=0),
    )(field, *[jnp.asarray(t) for t in tz + ty])


def power_kernel(b_ref, shell_ref, txh, txl, fold_ref, power_ref, sums_ref, total):
    plane = pl.program_id(0)
    nx, ny = b_ref.shape[2], b_ref.shape[3]

    @pl.when(plane == 0)
    def _():
        total[...] = jnp.zeros_like(total)

    data = halves(b_ref[0].reshape(2 * nx, ny))
    res = product((txh[...], txl[...]), data)
    power = jnp.square(res[:nx]) + jnp.square(res[nx:])
    power_ref[0] = power.T

    rows = 64

    def slab(i, carry):
        rs = pl.ds(pl.multiple_of(i * rows, rows), rows)
        marks = shell_ref[0, rs]
        upper, lower = halves(power_ref[0, rs])
        high = (marks // HALF).astype(F32).astype(BF16)
        low = (marks % HALF).astype(F32).astype(BF16)

        def wide(values):
            return jnp.concatenate([values[g * HALF : (g + 1) * HALF] for g in range(rows // HALF)], axis=1)

        upper, lower, high, low = wide(upper), wide(lower), wide(high), wide(low)
        zero = jnp.zeros_like(upper)
        one = jnp.ones_like(upper)
        a = [jnp.where(high == BF16(h), upper, zero) for h in range(HALF)]
        a += [jnp.where(high == BF16(h), lower, zero) for h in range(HALF)]
        b = [jnp.where(low == BF16(h), one, zero) for h in range(HALF)]
        total[...] += lax.dot_general(
            jnp.concatenate(a, axis=0),
            jnp.concatenate(b, axis=0),
            (((1,), (1,)), ((), ())),
            preferred_element_type=F32,
        )
        return carry

    lax.fori_loop(0, ny // rows, slab, 0)

    @pl.when(plane == pl.num_programs(0) - 1)
    def _():
        size = HALF * HALF
        both = total[:size] + total[size:]
        row = lax.broadcasted_iota(jnp.int32, (size, size), 0) % HALF
        col = lax.broadcasted_iota(jnp.int32, (size, size), 1) % HALF
        kept = jnp.where(row == col, both, 0.0).reshape(HALF, HALF, size)
        sums_ref[...] = jnp.dot(
            jnp.sum(kept, axis=1), fold_ref[...], precision=HIGH, preferred_element_type=F32
        )


def powers(b, shell):
    planes, _, nx, ny = b.shape
    cos_x, sin_x = waves(nx, np.arange(nx))
    cos_x, sin_x = cos_x.T, sin_x.T
    tx = two_parts(np.block([[cos_x, sin_x], [-sin_x, cos_x]]))
    fold = np.zeros((HALF * HALF, 128), np.float32)
    fold[np.arange(HALF * HALF), np.arange(HALF * HALF) // HALF] = 1.0
    whole = lambda shape: pl.BlockSpec(shape, lambda i: (0,) * len(shape))
    return pl.pallas_call(
        power_kernel,
        grid=(planes,),
        out_shape=[
            jax.ShapeDtypeStruct((planes, ny, nx), F32),
            jax.ShapeDtypeStruct((HALF, 128), F32),
        ],
        in_specs=[
            pl.BlockSpec((1, 2, nx, ny), lambda i: (i, 0, 0, 0)),
            pl.BlockSpec((1, ny, nx), lambda i: (i, 0, 0)),
            whole((2 * nx, 2 * nx)),
            whole((2 * nx, 2 * nx)),
            whole((HALF * HALF, 128)),
        ],
        out_specs=[pl.BlockSpec((1, ny, nx), lambda i: (i, 0, 0)), whole((HALF, 128))],
        scratch_shapes=[pltpu.VMEM((2 * HALF * HALF, HALF * HALF), F32)],
        compiler_params=pltpu.CompilerParams(vmem_limit_bytes=40 * MIB),
    )(b, shell, *[jnp.asarray(t) for t in tx], jnp.asarray(fold))


def sum_kernel(n_row, n_col, x_ref, o_ref, rcv1, mid, rcv2, s1, r1, s2, r2):
    my_row = lax.axis_index("row")
    my_col = lax.axis_index("col")
    greet(n_row, n_col, my_row, my_col)

    def row_copy(k):
        return pltpu.make_async_remote_copy(
            src_ref=x_ref,
            dst_ref=rcv1.at[my_row],
            send_sem=s1.at[k],
            recv_sem=r1.at[k],
            device_id={"row": lax.rem(my_row + k, n_row)},
            device_id_type=pl.DeviceIdType.MESH,
        )

    def col_copy(k):
        return pltpu.make_async_remote_copy(
            src_ref=mid,
            dst_ref=rcv2.at[my_col],
            send_sem=s2.at[k],
            recv_sem=r2.at[k],
            device_id={"col": lax.rem(my_col + k, n_col)},
            device_id_type=pl.DeviceIdType.MESH,
        )

    for k in range(1, n_row):
        row_copy(k).start()
    rcv1[my_row] = x_ref[...]
    for k in range(1, n_row):
        row_copy(k).wait_recv()
    mid[...] = jnp.sum(rcv1[...], axis=0)
    for k in range(1, n_col):
        col_copy(k).start()
    rcv2[my_col] = mid[...]
    for k in range(1, n_col):
        col_copy(k).wait_recv()
    o_ref[...] = jnp.sum(rcv2[...], axis=0)
    for k in range(1, n_row):
        row_copy(k).wait_send()
    for k in range(1, n_col):
        col_copy(k).wait_send()


def sum_all(x, n_row, n_col):
    vmem = pl.BlockSpec(memory_space=pltpu.VMEM)
    dma = pltpu.SemaphoreType.DMA
    return pl.pallas_call(
        functools.partial(sum_kernel, n_row, n_col),
        out_shape=jax.ShapeDtypeStruct(x.shape, F32),
        in_specs=[vmem],
        out_specs=vmem,
        scratch_shapes=[
            pltpu.VMEM((n_row,) + x.shape, F32),
            pltpu.VMEM(x.shape, F32),
            pltpu.VMEM((n_col,) + x.shape, F32),
            dma((n_row,)),
            dma((n_row,)),
            dma((n_col,)),
            dma((n_col,)),
        ],
        compiler_params=pltpu.CompilerParams(collective_id=1, has_side_effects=True),
    )(x)


def local(field, shell):
    fields, cx, cy, nz = field.shape
    n_row = lax.axis_size("row")
    n_col = lax.axis_size("col")
    nx, ny, keep = cx * n_row, cy * n_col, nz // 2
    planes = keep // (n_row * n_col)
    fits = fields == 1 and planes % 8 == 0 and (2 * keep // n_col) % 128 == 0
    fits = fits and cx % STEP == 0 and cy % 8 == 0 and nx % 128 == 0 and ny % 128 == 0
    if not fits:
        return general(field, shell)
    b = exchange(field.reshape(cx, cy, nz), n_row, n_col, planes)
    power, sums = powers(b, shell)
    sums = sum_all(sums, n_row, n_col)
    spectrum = sums[:, :HALF].reshape(1, SHELLS) * (float(SHELLS) / (keep * ny * nx))
    return (power.reshape(1, planes, ny, nx), spectrum)


def solution(mesh):
    in_specs = (P(None, "row", "col", None), P(("row", "col"), None, None))
    out_specs = (P(None, ("row", "col"), None, None), P())
    return jax.shard_map(local, mesh=mesh, in_specs=in_specs, out_specs=out_specs, check_vma=False)
```

```python
import math

import functools

import jax
import jax.numpy as jnp
import numpy as np
from jax import lax
from jax.experimental import pallas as pl
from jax.experimental.pallas import tpu as pltpu
from jax.sharding import PartitionSpec as P

SHELLS = 256


HIGH = lax.Precision.HIGHEST


def tables(length, freqs):
    places = lax.iota(jnp.int32, length)
    phase = places[:, None] * freqs[None, :] % length
    angle = phase.astype(jnp.float32) * (2.0 * math.pi / length)
    factor = 1.0 / math.sqrt(length)
    return (jnp.cos(angle) * factor, -jnp.sin(angle) * factor)


def split_three(values):
    upper = values.astype(jnp.bfloat16)
    upper_back = lax.optimization_barrier(upper).astype(jnp.float32)
    rest = values - upper_back
    middle = rest.astype(jnp.bfloat16)
    middle_back = lax.optimization_barrier(middle).astype(jnp.float32)
    lowest = (rest - middle_back).astype(jnp.bfloat16)
    return jnp.concatenate([upper, middle, lowest], axis=0)


def general(field, shell):
    fields, cx, cy, nz = field.shape
    n_row = lax.axis_size("row")
    n_col = lax.axis_size("col")
    nx = cx * n_row
    ny = cy * n_col
    keep = nz // 2
    planes = keep // (n_row * n_col)
    cos_x, sin_x = tables(nx, lax.iota(jnp.int32, nx))
    cos_y, sin_y = tables(ny, lax.iota(jnp.int32, ny))
    slots = lax.iota(jnp.int32, keep)
    col_block = slots // (n_row * planes)
    row_block = slots // planes % n_row
    inner = slots % planes
    freqs = (row_block * n_col + col_block) * planes + inner
    cos_z, sin_z = tables(nz, freqs)
    real = jnp.einsum("fxyz,zk->fxyk", field, cos_z, precision=HIGH)
    imag = jnp.einsum("fxyz,zk->fxyk", field, sin_z, precision=HIGH)
    cos_four = cos_y.reshape(n_col, cy, ny)
    sin_four = sin_y.reshape(n_col, cy, ny)
    a_re = lax.all_to_all(real, "col", split_axis=3, concat_axis=3, tiled=True)
    a_im = lax.all_to_all(imag, "col", split_axis=3, concat_axis=3, tiled=True)
    count = a_re.shape[1]
    a_re = a_re.reshape(fields, count, cy, n_col, keep // n_col)
    a_im = a_im.reshape(fields, count, cy, n_col, keep // n_col)
    o_re = jnp.einsum("fiasm,sak->fimk", a_re, cos_four, precision=HIGH) - jnp.einsum(
        "fiasm,sak->fimk", a_im, sin_four, precision=HIGH
    )
    o_im = jnp.einsum("fiasm,sak->fimk", a_re, sin_four, precision=HIGH) + jnp.einsum(
        "fiasm,sak->fimk", a_im, cos_four, precision=HIGH
    )
    real = o_re
    imag = o_im
    b_re = lax.all_to_all(real, "row", split_axis=2, concat_axis=1, tiled=True)
    b_im = lax.all_to_all(imag, "row", split_axis=2, concat_axis=1, tiled=True)
    o_re = jnp.einsum("fxpi,xk->fpik", b_re, cos_x, precision=HIGH) - jnp.einsum(
        "fxpi,xk->fpik", b_im, sin_x, precision=HIGH
    )
    o_im = jnp.einsum("fxpi,xk->fpik", b_re, sin_x, precision=HIGH) + jnp.einsum(
        "fxpi,xk->fpik", b_im, cos_x, precision=HIGH
    )
    power = o_re * o_re + o_im * o_im
    total = planes * ny * nx
    width = math.gcd(total, 32768)
    flat = power.reshape(fields, total)
    labels = shell.reshape(total)
    shell_ids = lax.iota(jnp.int32, SHELLS)

    def add_block(index, summed):
        start = index * width
        part = lax.dynamic_slice_in_dim(flat, start, width, 1)
        marks = lax.dynamic_slice_in_dim(labels, start, width, 0)
        onehot = (marks[:, None] == shell_ids[None, :]).astype(jnp.bfloat16)
        pieces = split_three(part)
        return summed + jnp.dot(pieces, onehot, preferred_element_type=jnp.float32)

    stacked = lax.fori_loop(
        0, total // width, add_block, jnp.zeros((3 * fields, SHELLS), jnp.float32)
    )
    sums = jnp.sum(stacked.reshape(3, fields, SHELLS), axis=0)
    sums = lax.psum(sums, ("row", "col"))
    spectrum = sums * (float(SHELLS) / (keep * ny * nx))
    return (power, spectrum)


F32 = jnp.float32
BF16 = jnp.bfloat16
MIB = 1 << 20
STEP = 8
SUB = 4
WINDOW = 3
HALF = 16


def waves(length, freqs):
    phase = np.arange(length)[:, None] * np.asarray(freqs)[None, :] % length
    angle = phase * (2.0 * np.pi / length)
    factor = 1.0 / math.sqrt(length)
    return np.cos(angle) * factor, np.sin(angle) * factor


def two_parts(table):
    upper = table.astype(np.float32).astype(jnp.bfloat16)
    lower = (table - upper.astype(np.float64)).astype(np.float32).astype(jnp.bfloat16)
    return upper, lower


def halves(values):
    upper = values.astype(BF16)
    return upper, (values - upper.astype(F32)).astype(BF16)


def dot(a, b):
    return jnp.dot(a, b, preferred_element_type=F32)


def product(a, b):
    return dot(a[0], b[0]) + (dot(a[1], b[0]) + dot(a[0], b[1]))


def greet(n_row, n_col, my_row, my_col):
    barrier = pltpu.get_barrier_semaphore()
    for k in range(1, n_col):
        pl.semaphore_signal(
            barrier, inc=1, device_id={"col": lax.rem(my_col + k, n_col)}, device_id_type=pl.DeviceIdType.MESH
        )
    for k in range(1, n_row):
        pl.semaphore_signal(
            barrier, inc=1, device_id={"row": lax.rem(my_row + k, n_row)}, device_id_type=pl.DeviceIdType.MESH
        )
    pl.semaphore_wait(barrier, n_col + n_row - 2)


def exchange_kernel(n_row, n_col, planes, f_hbm, tables_hbm, out_ref, scratch):
    f_ref, tzh, tzl, tyh, tyl, snd1, rcv1, snd2, s1, r1, s2, r2, own, f_sem, t_sem = scratch
    my_row = lax.axis_index("row")
    my_col = lax.axis_index("col")
    cx, cy, nz = f_ref.shape
    ny = cy * n_col
    width = rcv1.shape[3]
    half = width // 2
    steps = cx // STEP
    subs = cx // SUB
    loads = [
        pltpu.make_async_copy(src, dst, t_sem.at[i])
        for i, (src, dst) in enumerate(zip(tables_hbm, (tzh, tzl, tyh, tyl)))
    ]

    def field_copy(q):
        xs = pl.ds(q * STEP, STEP)
        return pltpu.make_async_copy(f_hbm.at[xs], f_ref.at[xs], f_sem.at[q])

    def col_copy(q, k):
        xs = pl.ds(q * SUB, SUB)
        dest = lax.rem(my_col + k, n_col)
        return pltpu.make_async_remote_copy(
            src_ref=snd1.at[dest, xs],
            dst_ref=rcv1.at[my_col, xs],
            send_sem=s1.at[q, k],
            recv_sem=r1.at[q, k],
            device_id={"col": dest},
            device_id_type=pl.DeviceIdType.MESH,
        )

    def row_copy(q, k):
        dest = lax.rem(my_row + k, n_row)
        there = pl.ds(pl.multiple_of(my_row * cx + q * STEP, STEP), STEP)
        return pltpu.make_async_remote_copy(
            src_ref=snd2.at[dest, :, :, pl.ds(pl.multiple_of(q * STEP, STEP), STEP)],
            dst_ref=out_ref.at[:, :, there],
            send_sem=s2.at[q, k],
            recv_sem=r2.at[q, k],
            device_id={"row": dest},
            device_id_type=pl.DeviceIdType.MESH,
        )

    def own_copy(q):
        there = pl.ds(pl.multiple_of(my_row * cx + q * STEP, STEP), STEP)
        return pltpu.make_async_copy(
            snd2.at[my_row, :, :, pl.ds(pl.multiple_of(q * STEP, STEP), STEP)], out_ref.at[:, :, there], own.at[q]
        )

    def col_start(j):
        for k in range(n_col - 1, 0, -1):
            col_copy(j, k).start()

    loads[0].start()
    loads[1].start()
    for q in range(steps):
        field_copy(q).start()
    loads[2].start()
    loads[3].start()
    greet(n_row, n_col, my_row, my_col)
    loads[0].wait()
    loads[1].wait()

    def depth_step(q, carry):
        field_copy(q).wait()
        xs = pl.ds(pl.multiple_of(q * STEP, STEP), STEP)
        data = halves(f_ref[xs].reshape(STEP * cy, nz))
        for c in range(n_col):
            cs = slice(c * width, (c + 1) * width)
            res = product(data, (tzh[:, cs], tzl[:, cs]))
            snd1[c, xs] = res.reshape(STEP, cy, width)
        for i in range(STEP // SUB):
            j = q * (STEP // SUB) + i

            @pl.when(j < WINDOW)
            def _():
                col_start(j)

        rcv1[my_col, xs] = snd1[my_col, xs]
        return carry

    lax.fori_loop(0, steps, depth_step, 0)
    loads[2].wait()
    loads[3].wait()

    def second_step(q, carry):
        for i in range(STEP // SUB):
            j = q * (STEP // SUB) + i
            for k in range(1, n_col):
                col_copy(j, k).wait_recv()

            @pl.when(j + WINDOW < subs)
            def _():
                col_start(j + WINDOW)

        parts = []
        for i in range(STEP):
            block = jnp.concatenate([rcv1[s, q * STEP + i] for s in range(n_col)], axis=0)
            parts.append(block.T)
        data = halves(jnp.concatenate(parts, axis=0))
        res = product(data, (tyh[...], tyl[...])).reshape(STEP, width, 2 * ny)
        real = res[:, :half, :ny] + res[:, half:, ny:]
        imag = res[:, half:, :ny] - res[:, :half, ny:]
        xs = pl.ds(pl.multiple_of(q * STEP, STEP), STEP)
        snd2[:, :, 0, xs] = jnp.swapaxes(real, 0, 1).reshape(n_row, planes, STEP, ny)
        snd2[:, :, 1, xs] = jnp.swapaxes(imag, 0, 1).reshape(n_row, planes, STEP, ny)
        for k in range(n_row - 1, 0, -1):
            row_copy(q, k).start()
        own_copy(q).start()
        return carry

    lax.fori_loop(0, steps, second_step, 0)

    def finish(q, carry):
        for i in range(STEP // SUB):
            for k in range(1, n_col):
                col_copy(q * (STEP // SUB) + i, k).wait_send()
        for k in range(1, n_row):
            row_copy(q, k).wait()
        own_copy(q).wait()
        return carry

    lax.fori_loop(0, steps, finish, 0)


def exchange(field, n_row, n_col, planes):
    cx, cy, nz = field.shape
    nx, ny, keep = cx * n_row, cy * n_col, nz // 2
    width = 2 * keep // n_col
    order = []
    for c in range(n_col):
        order.append([(r * n_col + c) * planes + p for r in range(n_row) for p in range(planes)])
    columns = []
    for freqs in order:
        cos_z, sin_z = waves(nz, freqs)
        columns += [cos_z, -sin_z]
    tz = two_parts(np.concatenate(columns, axis=1))
    ty = two_parts(np.concatenate(waves(ny, np.arange(ny)), axis=1))
    steps = cx // STEP
    dma = pltpu.SemaphoreType.DMA
    flops = 6 * (cx * cy * nz * 2 * keep + cx * width * ny * 2 * ny)
    subs = cx // SUB

    def body(f, a, b, c, d, out, *scratch):
        exchange_kernel(n_row, n_col, planes, f, (a, b, c, d), out, scratch)

    return pl.pallas_call(
        body,
        out_shape=jax.ShapeDtypeStruct((planes, 2, nx, ny), F32),
        in_specs=[pl.BlockSpec(memory_space=pl.ANY)] * 5,
        out_specs=pl.BlockSpec(memory_space=pl.ANY),
        scratch_shapes=[
            pltpu.VMEM((cx, cy, nz), F32),
            *[pltpu.VMEM(t.shape, BF16) for t in tz + ty],
            pltpu.VMEM((n_col, cx, cy, width), F32),
            pltpu.VMEM((n_col, cx, cy, width), F32),
            pltpu.VMEM((n_row, planes, 2, cx, ny), F32),
            dma((subs, n_col)),
            dma((subs, n_col)),
            dma((steps, n_row)),
            dma((steps, n_row)),
            dma((steps,)),
            dma((steps,)),
            dma((4,)),
        ],
        compiler_params=pltpu.CompilerParams(
            collective_id=0, has_side_effects=True, vmem_limit_bytes=60 * MIB
        ),
        cost_estimate=pl.CostEstimate(flops=flops, bytes_accessed=8 * cx * cy * nz, transcendentals=0),
    )(field, *[jnp.asarray(t) for t in tz + ty])


def power_kernel(scale, b_ref, shell_ref, txh, txl, fold_ref, power_ref, sums_ref, total):
    plane = pl.program_id(0)
    nx, ny = b_ref.shape[2], b_ref.shape[3]

    @pl.when(plane == 0)
    def _():
        total[...] = jnp.zeros_like(total)

    data = halves(b_ref[0].reshape(2 * nx, ny))
    res = product((txh[...], txl[...]), data)
    power = jnp.square(res[:nx]) + jnp.square(res[nx:])
    power_ref[0] = power.T

    rows = min(ny, 128)

    def slab(i, carry):
        rs = pl.ds(pl.multiple_of(i * rows, rows), rows)
        marks = shell_ref[0, rs]
        upper, lower = halves(power_ref[0, rs])
        high = (marks // HALF).astype(F32).astype(BF16)
        low = (marks % HALF).astype(F32).astype(BF16)

        def wide(values):
            return jnp.concatenate([values[g * HALF : (g + 1) * HALF] for g in range(rows // HALF)], axis=1)

        upper, lower, high, low = wide(upper), wide(lower), wide(high), wide(low)
        zero = jnp.zeros_like(upper)
        one = jnp.ones_like(upper)
        a = [jnp.where(high == BF16(h), upper, zero) for h in range(HALF)]
        a += [jnp.where(high == BF16(h), lower, zero) for h in range(HALF)]
        b = [jnp.where(low == BF16(h), one, zero) for h in range(HALF)]
        total[...] += lax.dot_general(
            jnp.concatenate(a, axis=0),
            jnp.concatenate(b, axis=0),
            (((1,), (1,)), ((), ())),
            preferred_element_type=F32,
        )
        return carry

    lax.fori_loop(0, ny // rows, slab, 0)

    @pl.when(plane == pl.num_programs(0) - 1)
    def _():
        size = HALF * HALF
        both = total[:size] + total[size:]
        row = lax.broadcasted_iota(jnp.int32, (size, size), 0) % HALF
        col = lax.broadcasted_iota(jnp.int32, (size, size), 1) % HALF
        kept = jnp.where(row == col, both, 0.0).reshape(HALF, HALF, size)
        folded = jnp.dot(
            jnp.sum(kept, axis=1), fold_ref[...], precision=HIGH, preferred_element_type=F32
        )
        at_high = lax.broadcasted_iota(jnp.int32, (HALF, size), 0)
        of_shell = lax.broadcasted_iota(jnp.int32, (HALF, size), 1) // HALF
        found = jnp.where(at_high == of_shell, folded, 0.0)
        sums_ref[...] = jnp.sum(found, axis=0, keepdims=True) * scale


def powers(b, shell, scale):
    planes, _, nx, ny = b.shape
    cos_x, sin_x = waves(nx, np.arange(nx))
    cos_x, sin_x = cos_x.T, sin_x.T
    tx = two_parts(np.block([[cos_x, sin_x], [-sin_x, cos_x]]))
    ids = np.arange(HALF * HALF)
    fold = (ids[:, None] // HALF == ids[None, :] % HALF).astype(np.float32)
    whole = lambda shape: pl.BlockSpec(shape, lambda i: (0,) * len(shape))
    return pl.pallas_call(
        functools.partial(power_kernel, scale),
        grid=(planes,),
        out_shape=[
            jax.ShapeDtypeStruct((planes, ny, nx), F32),
            jax.ShapeDtypeStruct((1, HALF * HALF), F32),
        ],
        in_specs=[
            pl.BlockSpec((1, 2, nx, ny), lambda i: (i, 0, 0, 0)),
            pl.BlockSpec((1, ny, nx), lambda i: (i, 0, 0)),
            whole((2 * nx, 2 * nx)),
            whole((2 * nx, 2 * nx)),
            whole((HALF * HALF, HALF * HALF)),
        ],
        out_specs=[pl.BlockSpec((1, ny, nx), lambda i: (i, 0, 0)), whole((1, HALF * HALF))],
        scratch_shapes=[pltpu.VMEM((2 * HALF * HALF, HALF * HALF), F32)],
        compiler_params=pltpu.CompilerParams(vmem_limit_bytes=60 * MIB),
    )(b, shell, *[jnp.asarray(t) for t in tx], jnp.asarray(fold))


def sum_kernel(n_row, n_col, x_ref, o_ref, rcv1, mid, rcv2, s1, r1, s2, r2):
    my_row = lax.axis_index("row")
    my_col = lax.axis_index("col")
    greet(n_row, n_col, my_row, my_col)

    def row_copy(k):
        return pltpu.make_async_remote_copy(
            src_ref=x_ref,
            dst_ref=rcv1.at[my_row],
            send_sem=s1.at[k],
            recv_sem=r1.at[k],
            device_id={"row": lax.rem(my_row + k, n_row)},
            device_id_type=pl.DeviceIdType.MESH,
        )

    def col_copy(k):
        return pltpu.make_async_remote_copy(
            src_ref=mid,
            dst_ref=rcv2.at[my_col],
            send_sem=s2.at[k],
            recv_sem=r2.at[k],
            device_id={"col": lax.rem(my_col + k, n_col)},
            device_id_type=pl.DeviceIdType.MESH,
        )

    for k in range(1, n_row):
        row_copy(k).start()
    rcv1[my_row] = x_ref[...]
    for k in range(1, n_row):
        row_copy(k).wait_recv()
    mid[...] = jnp.sum(rcv1[...], axis=0)
    for k in range(1, n_col):
        col_copy(k).start()
    rcv2[my_col] = mid[...]
    for k in range(1, n_col):
        col_copy(k).wait_recv()
    o_ref[...] = jnp.sum(rcv2[...], axis=0)
    for k in range(1, n_row):
        row_copy(k).wait_send()
    for k in range(1, n_col):
        col_copy(k).wait_send()


def sum_all(x, n_row, n_col):
    vmem = pl.BlockSpec(memory_space=pltpu.VMEM)
    dma = pltpu.SemaphoreType.DMA
    return pl.pallas_call(
        functools.partial(sum_kernel, n_row, n_col),
        out_shape=jax.ShapeDtypeStruct(x.shape, F32),
        in_specs=[vmem],
        out_specs=vmem,
        scratch_shapes=[
            pltpu.VMEM((n_row,) + x.shape, F32),
            pltpu.VMEM(x.shape, F32),
            pltpu.VMEM((n_col,) + x.shape, F32),
            dma((n_row,)),
            dma((n_row,)),
            dma((n_col,)),
            dma((n_col,)),
        ],
        compiler_params=pltpu.CompilerParams(collective_id=1, has_side_effects=True),
    )(x)


def local(field, shell):
    fields, cx, cy, nz = field.shape
    n_row = lax.axis_size("row")
    n_col = lax.axis_size("col")
    nx, ny, keep = cx * n_row, cy * n_col, nz // 2
    planes = keep // (n_row * n_col)
    fits = fields == 1 and planes % 8 == 0 and (2 * keep // n_col) % 128 == 0
    fits = fits and cx % STEP == 0 and cy % 8 == 0 and nx % 128 == 0 and ny % 128 == 0
    fits = fits and SHELLS == HALF * HALF
    if not fits:
        return general(field, shell)
    b = exchange(field.reshape(cx, cy, nz), n_row, n_col, planes)
    power, sums = powers(b, shell, float(SHELLS) / (keep * ny * nx))
    spectrum = sum_all(sums, n_row, n_col)
    return (power.reshape(1, planes, ny, nx), spectrum)


def solution(mesh):
    in_specs = (P(None, "row", "col", None), P(("row", "col"), None, None))
    out_specs = (P(None, ("row", "col"), None, None), P())
    return jax.shard_map(local, mesh=mesh, in_specs=in_specs, out_specs=out_specs, check_vma=False)
```

```python
import math

import functools

import jax
import jax.numpy as jnp
import numpy as np
from jax import lax
from jax.experimental import pallas as pl
from jax.experimental.pallas import tpu as pltpu
from jax.sharding import PartitionSpec as P

SHELLS = 256


HIGH = lax.Precision.HIGHEST


def tables(length, freqs):
    places = lax.iota(jnp.int32, length)
    phase = places[:, None] * freqs[None, :] % length
    angle = phase.astype(jnp.float32) * (2.0 * math.pi / length)
    factor = 1.0 / math.sqrt(length)
    return (jnp.cos(angle) * factor, -jnp.sin(angle) * factor)


def split_three(values):
    upper = values.astype(jnp.bfloat16)
    upper_back = lax.optimization_barrier(upper).astype(jnp.float32)
    rest = values - upper_back
    middle = rest.astype(jnp.bfloat16)
    middle_back = lax.optimization_barrier(middle).astype(jnp.float32)
    lowest = (rest - middle_back).astype(jnp.bfloat16)
    return jnp.concatenate([upper, middle, lowest], axis=0)


def general(field, shell):
    fields, cx, cy, nz = field.shape
    n_row = lax.axis_size("row")
    n_col = lax.axis_size("col")
    nx = cx * n_row
    ny = cy * n_col
    keep = nz // 2
    planes = keep // (n_row * n_col)
    cos_x, sin_x = tables(nx, lax.iota(jnp.int32, nx))
    cos_y, sin_y = tables(ny, lax.iota(jnp.int32, ny))
    slots = lax.iota(jnp.int32, keep)
    col_block = slots // (n_row * planes)
    row_block = slots // planes % n_row
    inner = slots % planes
    freqs = (row_block * n_col + col_block) * planes + inner
    cos_z, sin_z = tables(nz, freqs)
    real = jnp.einsum("fxyz,zk->fxyk", field, cos_z, precision=HIGH)
    imag = jnp.einsum("fxyz,zk->fxyk", field, sin_z, precision=HIGH)
    cos_four = cos_y.reshape(n_col, cy, ny)
    sin_four = sin_y.reshape(n_col, cy, ny)
    a_re = lax.all_to_all(real, "col", split_axis=3, concat_axis=3, tiled=True)
    a_im = lax.all_to_all(imag, "col", split_axis=3, concat_axis=3, tiled=True)
    count = a_re.shape[1]
    a_re = a_re.reshape(fields, count, cy, n_col, keep // n_col)
    a_im = a_im.reshape(fields, count, cy, n_col, keep // n_col)
    o_re = jnp.einsum("fiasm,sak->fimk", a_re, cos_four, precision=HIGH) - jnp.einsum(
        "fiasm,sak->fimk", a_im, sin_four, precision=HIGH
    )
    o_im = jnp.einsum("fiasm,sak->fimk", a_re, sin_four, precision=HIGH) + jnp.einsum(
        "fiasm,sak->fimk", a_im, cos_four, precision=HIGH
    )
    real = o_re
    imag = o_im
    b_re = lax.all_to_all(real, "row", split_axis=2, concat_axis=1, tiled=True)
    b_im = lax.all_to_all(imag, "row", split_axis=2, concat_axis=1, tiled=True)
    o_re = jnp.einsum("fxpi,xk->fpik", b_re, cos_x, precision=HIGH) - jnp.einsum(
        "fxpi,xk->fpik", b_im, sin_x, precision=HIGH
    )
    o_im = jnp.einsum("fxpi,xk->fpik", b_re, sin_x, precision=HIGH) + jnp.einsum(
        "fxpi,xk->fpik", b_im, cos_x, precision=HIGH
    )
    power = o_re * o_re + o_im * o_im
    total = planes * ny * nx
    width = math.gcd(total, 32768)
    flat = power.reshape(fields, total)
    labels = shell.reshape(total)
    shell_ids = lax.iota(jnp.int32, SHELLS)

    def add_block(index, summed):
        start = index * width
        part = lax.dynamic_slice_in_dim(flat, start, width, 1)
        marks = lax.dynamic_slice_in_dim(labels, start, width, 0)
        onehot = (marks[:, None] == shell_ids[None, :]).astype(jnp.bfloat16)
        pieces = split_three(part)
        return summed + jnp.dot(pieces, onehot, preferred_element_type=jnp.float32)

    stacked = lax.fori_loop(
        0, total // width, add_block, jnp.zeros((3 * fields, SHELLS), jnp.float32)
    )
    sums = jnp.sum(stacked.reshape(3, fields, SHELLS), axis=0)
    sums = lax.psum(sums, ("row", "col"))
    spectrum = sums * (float(SHELLS) / (keep * ny * nx))
    return (power, spectrum)


F32 = jnp.float32
BF16 = jnp.bfloat16
MIB = 1 << 20
STEP = 8
SUB = 4
WINDOW = 2
HALF = 16


def waves(length, freqs):
    phase = np.arange(length)[:, None] * np.asarray(freqs)[None, :] % length
    angle = phase * (2.0 * np.pi / length)
    factor = 1.0 / math.sqrt(length)
    return np.cos(angle) * factor, np.sin(angle) * factor


def two_parts(table):
    upper = table.astype(np.float32).astype(jnp.bfloat16)
    lower = (table - upper.astype(np.float64)).astype(np.float32).astype(jnp.bfloat16)
    return upper, lower


def halves(values):
    upper = values.astype(BF16)
    return upper, (values - upper.astype(F32)).astype(BF16)


def dot(a, b):
    return jnp.dot(a, b, preferred_element_type=F32)


def product(a, b):
    return dot(a[0], b[0]) + (dot(a[1], b[0]) + dot(a[0], b[1]))


def greet(n_row, n_col, my_row, my_col):
    barrier = pltpu.get_barrier_semaphore()
    for k in range(1, n_col):
        pl.semaphore_signal(
            barrier, inc=1, device_id={"col": lax.rem(my_col + k, n_col)}, device_id_type=pl.DeviceIdType.MESH
        )
    for k in range(1, n_row):
        pl.semaphore_signal(
            barrier, inc=1, device_id={"row": lax.rem(my_row + k, n_row)}, device_id_type=pl.DeviceIdType.MESH
        )
    pl.semaphore_wait(barrier, n_col + n_row - 2)


def exchange_kernel(n_row, n_col, planes, f_hbm, tables_hbm, out_ref, scratch):
    f_ref, tzh, tzl, tyh, tyl, snd1, rcv1, snd2, s1, r1, s2, r2, own, f_sem, t_sem = scratch
    my_row = lax.axis_index("row")
    my_col = lax.axis_index("col")
    cx, cy, nz = f_ref.shape
    ny = cy * n_col
    width = rcv1.shape[3]
    half = width // 2
    steps = cx // STEP
    subs = cx // SUB
    loads = [
        pltpu.make_async_copy(src, dst, t_sem.at[i])
        for i, (src, dst) in enumerate(zip(tables_hbm, (tzh, tzl, tyh, tyl)))
    ]

    def field_copy(q):
        xs = pl.ds(q * STEP, STEP)
        return pltpu.make_async_copy(f_hbm.at[xs], f_ref.at[xs], f_sem.at[q])

    def col_copy(q, k):
        xs = pl.ds(q * SUB, SUB)
        dest = lax.rem(my_col + k, n_col)
        return pltpu.make_async_remote_copy(
            src_ref=snd1.at[dest, xs],
            dst_ref=rcv1.at[my_col, xs],
            send_sem=s1.at[q, k],
            recv_sem=r1.at[q, k],
            device_id={"col": dest},
            device_id_type=pl.DeviceIdType.MESH,
        )

    def row_copy(q, k):
        dest = lax.rem(my_row + k, n_row)
        there = pl.ds(pl.multiple_of(my_row * cx + q * STEP, STEP), STEP)
        return pltpu.make_async_remote_copy(
            src_ref=snd2.at[dest, :, :, pl.ds(pl.multiple_of(q * STEP, STEP), STEP)],
            dst_ref=out_ref.at[:, :, there],
            send_sem=s2.at[q, k],
            recv_sem=r2.at[q, k],
            device_id={"row": dest},
            device_id_type=pl.DeviceIdType.MESH,
        )

    def own_copy(q):
        there = pl.ds(pl.multiple_of(my_row * cx + q * STEP, STEP), STEP)
        return pltpu.make_async_copy(
            snd2.at[my_row, :, :, pl.ds(pl.multiple_of(q * STEP, STEP), STEP)], out_ref.at[:, :, there], own.at[q]
        )

    def col_start(j):
        for k in range(n_col - 1, 0, -1):
            col_copy(j, k).start()

    loads[0].start()
    loads[1].start()
    for q in range(steps):
        field_copy(q).start()
    loads[2].start()
    loads[3].start()
    greet(n_row, n_col, my_row, my_col)
    loads[0].wait()
    loads[1].wait()

    def depth_step(q, carry):
        field_copy(q).wait()
        xs = pl.ds(pl.multiple_of(q * STEP, STEP), STEP)
        data = halves(f_ref[xs].reshape(STEP * cy, nz))
        for c in range(n_col):
            cs = slice(c * width, (c + 1) * width)
            res = product(data, (tzh[:, cs], tzl[:, cs]))
            snd1[c, xs] = res.reshape(STEP, cy, width)
        for i in range(STEP // SUB):
            j = q * (STEP // SUB) + i

            @pl.when(j < WINDOW)
            def _():
                col_start(j)

        rcv1[my_col, xs] = snd1[my_col, xs]
        return carry

    lax.fori_loop(0, steps, depth_step, 0)
    loads[2].wait()
    loads[3].wait()

    def second_step(q, carry):
        for i in range(STEP // SUB):
            j = q * (STEP // SUB) + i
            for k in range(1, n_col):
                col_copy(j, k).wait_recv()

            @pl.when(j + WINDOW < subs)
            def _():
                col_start(j + WINDOW)

        parts = []
        for i in range(STEP):
            block = jnp.concatenate([rcv1[s, q * STEP + i] for s in range(n_col)], axis=0)
            parts.append(block.T)
        data = halves(jnp.concatenate(parts, axis=0))
        res = product(data, (tyh[...], tyl[...])).reshape(STEP, width, 2 * ny)
        real = res[:, :half, :ny] + res[:, half:, ny:]
        imag = res[:, half:, :ny] - res[:, :half, ny:]
        xs = pl.ds(pl.multiple_of(q * STEP, STEP), STEP)
        snd2[:, :, 0, xs] = jnp.swapaxes(real, 0, 1).reshape(n_row, planes, STEP, ny)
        snd2[:, :, 1, xs] = jnp.swapaxes(imag, 0, 1).reshape(n_row, planes, STEP, ny)
        for k in range(n_row - 1, 0, -1):
            row_copy(q, k).start()
        own_copy(q).start()
        return carry

    lax.fori_loop(0, steps, second_step, 0)

    def finish(q, carry):
        for i in range(STEP // SUB):
            for k in range(1, n_col):
                col_copy(q * (STEP // SUB) + i, k).wait_send()
        for k in range(1, n_row):
            row_copy(q, k).wait()
        own_copy(q).wait()
        return carry

    lax.fori_loop(0, steps, finish, 0)


def exchange(field, n_row, n_col, planes):
    cx, cy, nz = field.shape
    nx, ny, keep = cx * n_row, cy * n_col, nz // 2
    width = 2 * keep // n_col
    order = []
    for c in range(n_col):
        order.append([(r * n_col + c) * planes + p for r in range(n_row) for p in range(planes)])
    columns = []
    for freqs in order:
        cos_z, sin_z = waves(nz, freqs)
        columns += [cos_z, -sin_z]
    tz = two_parts(np.concatenate(columns, axis=1))
    ty = two_parts(np.concatenate(waves(ny, np.arange(ny)), axis=1))
    steps = cx // STEP
    dma = pltpu.SemaphoreType.DMA
    flops = 6 * (cx * cy * nz * 2 * keep + cx * width * ny * 2 * ny)
    subs = cx // SUB

    def body(f, a, b, c, d, out, *scratch):
        exchange_kernel(n_row, n_col, planes, f, (a, b, c, d), out, scratch)

    return pl.pallas_call(
        body,
        out_shape=jax.ShapeDtypeStruct((planes, 2, nx, ny), F32),
        in_specs=[pl.BlockSpec(memory_space=pl.ANY)] * 5,
        out_specs=pl.BlockSpec(memory_space=pl.ANY),
        scratch_shapes=[
            pltpu.VMEM((cx, cy, nz), F32),
            *[pltpu.VMEM(t.shape, BF16) for t in tz + ty],
            pltpu.VMEM((n_col, cx, cy, width), F32),
            pltpu.VMEM((n_col, cx, cy, width), F32),
            pltpu.VMEM((n_row, planes, 2, cx, ny), F32),
            dma((subs, n_col)),
            dma((subs, n_col)),
            dma((steps, n_row)),
            dma((steps, n_row)),
            dma((steps,)),
            dma((steps,)),
            dma((4,)),
        ],
        compiler_params=pltpu.CompilerParams(
            collective_id=0, has_side_effects=True, vmem_limit_bytes=60 * MIB
        ),
        cost_estimate=pl.CostEstimate(flops=flops, bytes_accessed=8 * cx * cy * nz, transcendentals=0),
    )(field, *[jnp.asarray(t) for t in tz + ty])


def power_kernel(scale, b_ref, shell_ref, txh, txl, fold_ref, power_ref, sums_ref, total):
    plane = pl.program_id(0)
    nx, ny = b_ref.shape[2], b_ref.shape[3]

    @pl.when(plane == 0)
    def _():
        total[...] = jnp.zeros_like(total)

    data = halves(b_ref[0].reshape(2 * nx, ny))
    res = product((txh[...], txl[...]), data)
    power = jnp.square(res[:nx]) + jnp.square(res[nx:])
    power_ref[0] = power.T

    rows = min(ny, 256)

    def slab(i, carry):
        rs = pl.ds(pl.multiple_of(i * rows, rows), rows)
        marks = shell_ref[0, rs]
        upper, lower = halves(power_ref[0, rs])
        high = (marks // HALF).astype(F32).astype(BF16)
        low = (marks % HALF).astype(F32).astype(BF16)

        def wide(values):
            return jnp.concatenate([values[g * HALF : (g + 1) * HALF] for g in range(rows // HALF)], axis=1)

        upper, lower, high, low = wide(upper), wide(lower), wide(high), wide(low)
        zero = jnp.zeros_like(upper)
        one = jnp.ones_like(upper)
        a = [jnp.where(high == BF16(h), upper, zero) for h in range(HALF)]
        a += [jnp.where(high == BF16(h), lower, zero) for h in range(HALF)]
        b = [jnp.where(low == BF16(h), one, zero) for h in range(HALF)]
        total[...] += lax.dot_general(
            jnp.concatenate(a, axis=0),
            jnp.concatenate(b, axis=0),
            (((1,), (1,)), ((), ())),
            preferred_element_type=F32,
        )
        return carry

    lax.fori_loop(0, ny // rows, slab, 0)

    @pl.when(plane == pl.num_programs(0) - 1)
    def _():
        size = HALF * HALF
        both = total[:size] + total[size:]
        row = lax.broadcasted_iota(jnp.int32, (size, size), 0) % HALF
        col = lax.broadcasted_iota(jnp.int32, (size, size), 1) % HALF
        kept = jnp.where(row == col, both, 0.0).reshape(HALF, HALF, size)
        folded = jnp.dot(
            jnp.sum(kept, axis=1), fold_ref[...], precision=HIGH, preferred_element_type=F32
        )
        at_high = lax.broadcasted_iota(jnp.int32, (HALF, size), 0)
        of_shell = lax.broadcasted_iota(jnp.int32, (HALF, size), 1) // HALF
        found = jnp.where(at_high == of_shell, folded, 0.0)
        sums_ref[...] = jnp.sum(found, axis=0, keepdims=True) * scale


def powers(b, shell, scale):
    planes, _, nx, ny = b.shape
    cos_x, sin_x = waves(nx, np.arange(nx))
    cos_x, sin_x = cos_x.T, sin_x.T
    tx = two_parts(np.block([[cos_x, sin_x], [-sin_x, cos_x]]))
    ids = np.arange(HALF * HALF)
    fold = (ids[:, None] // HALF == ids[None, :] % HALF).astype(np.float32)
    whole = lambda shape: pl.BlockSpec(shape, lambda i: (0,) * len(shape))
    return pl.pallas_call(
        functools.partial(power_kernel, scale),
        grid=(planes,),
        out_shape=[
            jax.ShapeDtypeStruct((planes, ny, nx), F32),
            jax.ShapeDtypeStruct((1, HALF * HALF), F32),
        ],
        in_specs=[
            pl.BlockSpec((1, 2, nx, ny), lambda i: (i, 0, 0, 0)),
            pl.BlockSpec((1, ny, nx), lambda i: (i, 0, 0)),
            whole((2 * nx, 2 * nx)),
            whole((2 * nx, 2 * nx)),
            whole((HALF * HALF, HALF * HALF)),
        ],
        out_specs=[pl.BlockSpec((1, ny, nx), lambda i: (i, 0, 0)), whole((1, HALF * HALF))],
        scratch_shapes=[pltpu.VMEM((2 * HALF * HALF, HALF * HALF), F32)],
        compiler_params=pltpu.CompilerParams(vmem_limit_bytes=60 * MIB),
    )(b, shell, *[jnp.asarray(t) for t in tx], jnp.asarray(fold))


def sum_kernel(n_row, n_col, x_ref, o_ref, rcv1, mid, rcv2, s1, r1, s2, r2):
    my_row = lax.axis_index("row")
    my_col = lax.axis_index("col")
    greet(n_row, n_col, my_row, my_col)

    def row_copy(k):
        return pltpu.make_async_remote_copy(
            src_ref=x_ref,
            dst_ref=rcv1.at[my_row],
            send_sem=s1.at[k],
            recv_sem=r1.at[k],
            device_id={"row": lax.rem(my_row + k, n_row)},
            device_id_type=pl.DeviceIdType.MESH,
        )

    def col_copy(k):
        return pltpu.make_async_remote_copy(
            src_ref=mid,
            dst_ref=rcv2.at[my_col],
            send_sem=s2.at[k],
            recv_sem=r2.at[k],
            device_id={"col": lax.rem(my_col + k, n_col)},
            device_id_type=pl.DeviceIdType.MESH,
        )

    for k in range(1, n_row):
        row_copy(k).start()
    rcv1[my_row] = x_ref[...]
    for k in range(1, n_row):
        row_copy(k).wait_recv()
    mid[...] = jnp.sum(rcv1[...], axis=0)
    for k in range(1, n_col):
        col_copy(k).start()
    rcv2[my_col] = mid[...]
    for k in range(1, n_col):
        col_copy(k).wait_recv()
    o_ref[...] = jnp.sum(rcv2[...], axis=0)
    for k in range(1, n_row):
        row_copy(k).wait_send()
    for k in range(1, n_col):
        col_copy(k).wait_send()


def sum_all(x, n_row, n_col):
    vmem = pl.BlockSpec(memory_space=pltpu.VMEM)
    dma = pltpu.SemaphoreType.DMA
    return pl.pallas_call(
        functools.partial(sum_kernel, n_row, n_col),
        out_shape=jax.ShapeDtypeStruct(x.shape, F32),
        in_specs=[vmem],
        out_specs=vmem,
        scratch_shapes=[
            pltpu.VMEM((n_row,) + x.shape, F32),
            pltpu.VMEM(x.shape, F32),
            pltpu.VMEM((n_col,) + x.shape, F32),
            dma((n_row,)),
            dma((n_row,)),
            dma((n_col,)),
            dma((n_col,)),
        ],
        compiler_params=pltpu.CompilerParams(collective_id=1, has_side_effects=True),
    )(x)


def local(field, shell):
    fields, cx, cy, nz = field.shape
    n_row = lax.axis_size("row")
    n_col = lax.axis_size("col")
    nx, ny, keep = cx * n_row, cy * n_col, nz // 2
    planes = keep // (n_row * n_col)
    fits = fields == 1 and planes % 8 == 0 and (2 * keep // n_col) % 128 == 0
    fits = fits and cx % STEP == 0 and cy % 8 == 0 and nx % 128 == 0 and ny % 128 == 0
    fits = fits and SHELLS == HALF * HALF and ny % min(ny, 256) == 0
    if not fits:
        return general(field, shell)
    b = exchange(field.reshape(cx, cy, nz), n_row, n_col, planes)
    power, sums = powers(b, shell, float(SHELLS) / (keep * ny * nx))
    spectrum = sum_all(sums, n_row, n_col)
    return (power.reshape(1, planes, ny, nx), spectrum)


def solution(mesh):
    in_specs = (P(None, "row", "col", None), P(("row", "col"), None, None))
    out_specs = (P(None, ("row", "col"), None, None), P())
    return jax.shard_map(local, mesh=mesh, in_specs=in_specs, out_specs=out_specs, check_vma=False)
```
